512 devices in a mesh: ctx: 64 (over z_hi, y, x, core), head: 8 (over z_lo).
Axes of the slice: x: 4, y: 4, z: 16 (z_hi: 2, z_lo: 8; z = z_hi * 8 + z_lo), core: 2. Of those that a mesh axis runs over, the one named last changes fastest.
Arguments:
- queries: bfloat16 [4096, 8192], P('ctx', 'head'), may hold values from -7 to 7
- suffix_key_rows: bfloat16 [4096, 1024], P('ctx', 'head'), may hold values from -6 to 6
- suffix_value_rows: bfloat16 [4096, 1024], P('ctx', 'head'), may hold values from -6 to 6
- prefix_key_slots: bfloat16 [20480, 1024], P('ctx', 'head'), may hold values from -6 to 6
- prefix_value_slots: bfloat16 [20480, 1024], P('ctx', 'head'), may hold values from -6 to 6
- pool_counts: int32 [64], replicated, may hold values from 1 to 320, 10240 in all
- span_order: int32 [64], replicated, may hold values from 0 to 63, each once
Outputs:
- context: bfloat16 [4096, 8192], P(('ctx', 'head'))
The draws below stay inside these ranges and needn't reach their ends.
Inputs may be any that keep to these rules, and one draw needn't show every extreme that they name: `pool_counts`: positive; the counts sum to 10240 and the largest is 320. `span_order`: each block number once.
All inputs are finite; a program needn't handle non-finite values.
Results may differ from the reference program's by a relative error of at most 0.01.
Values may be sent and summed in bfloat16 or wider, within the bound.
A program may use at most 64 MiB of HBM per device.

```python
import math
import jax
import jax.numpy as jnp
import numpy as np
from jax import lax

QUERY_HEADS = 64
KEY_HEADS = 8
HEAD_SIZE = 128
SUF_DEV = 64
HEADS_PER_KEY = 8
POOL_DEV = 320
PREFIX = 10240
POOL_SLOT_COUNT = 20480
SUFFIX_TOKENS = 4096
N_CTX = 64


def draw_queries(key, part):
    key = jax.random.fold_in(key, 7)
    value_rows = jnp.clip(jax.random.normal(key, (SUFFIX_TOKENS, QUERY_HEADS, HEAD_SIZE), jnp.float32), -6.0, 6.0)
    return value_rows.reshape(SUFFIX_TOKENS, QUERY_HEADS * HEAD_SIZE).astype(jnp.bfloat16)


def draw_prefix_key_slots(key, part):
    key = jax.random.fold_in(key, 9)
    value_rows = jnp.clip(jax.random.normal(key, (POOL_SLOT_COUNT, KEY_HEADS, HEAD_SIZE), jnp.float32), -6.0, 6.0)
    return value_rows.reshape(POOL_SLOT_COUNT, KEY_HEADS * HEAD_SIZE).astype(jnp.bfloat16)


def steps_of(stream_key, dims, pieces, smallest, largest):
    loudness, own = 1.0, jax.random.fold_in(stream_key, 6)
    for axis_at, parts in pieces:
        steps = jnp.exp(jax.random.uniform(jax.random.fold_in(own, axis_at), (parts,), jnp.float32, smallest / len(pieces), largest / len(pieces)))
        loudness = loudness * jnp.repeat(steps, dims[axis_at] // parts).reshape([-1 if axis == axis_at else 1 for axis in range(len(dims))])
    return loudness


def profile(number_of, total, limit, slope):
    portions = [(1 << 20) // math.isqrt(rank ** slope) + 1 for rank in range(2, number_of + 1)]
    spare, counts = total - limit - (number_of - 1), [1] * (number_of - 1)
    while spare > 0:
        free = [i for i in range(number_of - 1) if counts[i] < limit]
        pool, remaining = sum([portions[i] for i in free]), spare
        for i in free:
            extra = min(limit - counts[i], max(1, remaining * portions[i] // pool), spare)
            counts[i] = counts[i] + extra
            spare = spare - extra
    return np.array([limit] + counts)


def uneven_parts(own_key, number_of, total, limit, slope):
    if number_of == 2:
        one = jax.random.randint(own_key, (), max(1, total - limit), min(limit, total - 1) + 1)
        return jnp.stack([one, total - one])
    sizes = jnp.asarray(profile(number_of, total, limit, slope), jnp.int32)
    couples = (number_of - 1) // 2
    source_of, sink = sizes[1:1 + 2 * couples:2], sizes[2:2 + 2 * couples:2]
    margin = jnp.minimum(source_of - 1, limit - sink)
    shifted = jax.random.randint(jax.random.fold_in(own_key, 1), (couples,), 0, 1 << 20) % (margin + 1)
    sizes = sizes.at[1:1 + 2 * couples:2].set(source_of - shifted).at[2:2 + 2 * couples:2].set(sink + shifted)
    return sizes[jax.random.permutation(jax.random.fold_in(own_key, 2), number_of)]


def gaussian(own_key, dims, spread, reach, pieces=(), kind=jnp.bfloat16):
    loudness = steps_of(own_key, dims, pieces, -0.22, 0.18) if pieces else 1.0
    values = jax.random.normal(own_key, dims, jnp.float32) * spread * loudness
    return jnp.minimum(jnp.maximum(values, -reach), reach).astype(kind)


def setup_inputs(seed: int = 0) -> dict:
    key_of = jax.random.split(jax.random.key(seed), 8)
    return {
        "queries": draw_queries(jax.random.fold_in(key_of[7], 71), 0),
        "suffix_key_rows": gaussian(key_of[1], (SUFFIX_TOKENS, KEY_HEADS * HEAD_SIZE), 1.0, 6.0, ((0, 64), (1, 8))),
        "suffix_value_rows": gaussian(key_of[2], (SUFFIX_TOKENS, KEY_HEADS * HEAD_SIZE), 1.0, 6.0, ((0, 64), (1, 8))),
        "prefix_key_slots": draw_prefix_key_slots(jax.random.fold_in(key_of[7], 71), 0),
        "prefix_value_slots": gaussian(key_of[4], (POOL_SLOT_COUNT, KEY_HEADS * HEAD_SIZE), 1.0, 6.0, ((0, 64), (1, 8))),
        "pool_counts": uneven_parts(key_of[5], N_CTX, PREFIX, POOL_DEV, 2).astype(jnp.int32),
        "span_order": jax.random.permutation(key_of[6], N_CTX).astype(jnp.int32),
    }


hidden_mark = 1073741824

def reference(queries, suffix_key_rows, suffix_value_rows, prefix_key_slots, prefix_value_slots, pool_counts, span_order):
    qpos = (jnp.repeat(span_order, SUF_DEV) * SUF_DEV + jnp.tile(jnp.arange(SUF_DEV, dtype=jnp.int32), N_CTX)).astype(jnp.int32)
    slots = jnp.arange(POOL_SLOT_COUNT, dtype=jnp.int32)
    live = slots % POOL_DEV < pool_counts[slots // POOL_DEV]
    kpos = jnp.concatenate([jnp.where(live, -1, hidden_mark).astype(jnp.int32), qpos]).astype(jnp.int32)
    key_rows = jnp.concatenate([prefix_key_slots, suffix_key_rows]).reshape(-1, KEY_HEADS, HEAD_SIZE).transpose(1, 0, 2)
    value_rows = jnp.concatenate([prefix_value_slots, suffix_value_rows]).reshape(-1, KEY_HEADS, HEAD_SIZE).transpose(1, 0, 2)
    query_heads = queries.reshape(SUFFIX_TOKENS, KEY_HEADS, HEADS_PER_KEY, HEAD_SIZE).transpose(1, 0, 2, 3)
    qblock = math.gcd(SUFFIX_TOKENS, 128)
    count = SUFFIX_TOKENS // qblock
    scale = 1.0 / math.sqrt(HEAD_SIZE)
    qpos_blocks = qpos.reshape(count, qblock)

    def per_head(operands):
        head_q, head_k, head_v = operands
        kf = head_k.astype(jnp.float32)
        vf = head_v.astype(jnp.float32)

        def per_block(inner):
            qb, qp = inner
            s = jnp.einsum('sgd,pd->gsp', qb.astype(jnp.float32), kf) * scale
            mask = kpos[None, None, :] <= qp[None, :, None]
            s = jnp.where(mask, s, -1e+30)
            top = lax.optimization_barrier(jnp.max(s, axis=-1))
            p = jnp.where(mask, jnp.exp(s - top[..., None]), 0.0)
            total = lax.optimization_barrier(jnp.sum(p, axis=-1))
            pb = lax.optimization_barrier(p.astype(jnp.bfloat16)).astype(jnp.float32)
            o = jnp.einsum('gsp,pd->sgd', pb, vf) / total.T[..., None]
            return o.astype(jnp.bfloat16)
        return lax.map(per_block, (head_q.reshape(count, qblock, HEADS_PER_KEY, HEAD_SIZE), qpos_blocks))
    result = lax.map(per_head, (query_heads, key_rows, value_rows))
    return result.transpose(1, 2, 0, 3, 4).reshape(SUFFIX_TOKENS, QUERY_HEADS * HEAD_SIZE)
```

```python
import math

import jax
import jax.numpy as jnp
from jax import lax
from jax.experimental import pallas as pl
from jax.experimental.pallas import tpu as pltpu
from jax.sharding import PartitionSpec as P

HEAD = 128
GROUP = 8
SUF = 64
POOL = 320
KEYS = POOL + SUF
WIDE = 2 * KEYS
VROWS = 144
COLS = SUF * GROUP
MSG = 80
SIDE = 4
HEADS = 8
NEG = -1e30
FACTOR = math.log2(math.e) / math.sqrt(HEAD)
MESH = pl.DeviceIdType.MESH


def kernel(
    q_ref, k_ref, vt_ref, span_ref, out_ref,
    kbuf, vbuf, qraw, qbuf, sbuf, acc, top, send, land, weights,
    s_first, r_first, s_line, r_line, s_core, r_core, s_q, r_q, s_out, r_out, s_own,
):
    ctx, zl = lax.axis_index("ctx"), lax.axis_index("head")
    c = ctx % 2
    x = ctx // 2 % SIDE
    y = ctx // (2 * SIDE) % SIDE
    zh = ctx // (2 * SIDE * SIDE)
    u = y * (1 - c) + x * c
    w = x * (1 - c) + y * c

    def place(plane, first, second, core):
        row = first * (1 - core) + second * core
        col = second * (1 - core) + first * core
        return ((plane * SIDE + row) * SIDE + col) * 2 + core

    def first(step):
        return (place(zh, (u + step) % SIDE, w, c), zl)

    def second(step):
        return (place(zh, u, (w + step) % SIDE, c), zl)

    partner = (ctx + 1 - 2 * c, zl)
    across = (place(1 - zh, u, w, c), zl)

    def column(flip, step):
        plane = (zh + flip) % 2
        return (place(plane, u, w, c), (zl + step) % HEADS)

    far = [(flip, step) for flip in (1, 0) for step in (4, 3, 5, 2, 6, 1, 7, 0) if flip or step]

    barrier = pltpu.get_barrier_semaphore()
    greeted = [column(f, s) for f, s in far]
    greeted += [first(1), first(2), first(3), second(1), second(3), partner]
    for who in greeted:
        pl.semaphore_signal(barrier, inc=1, device_id=who, device_id_type=MESH)

    def remote(src, dst, s_sem, r_sem, who):
        return pltpu.make_async_remote_copy(
            src_ref=src, dst_ref=dst, send_sem=s_sem, recv_sem=r_sem,
            device_id=who, device_id_type=MESH,
        )

    own_k = pltpu.make_async_copy(k_ref, kbuf.at[0, 0, pl.ds(0, KEYS)], s_own.at[0])
    own_v = pltpu.make_async_copy(vt_ref, vbuf.at[0, 0, :, pl.ds(0, KEYS)], s_own.at[1])
    own_k.start()
    own_v.start()

    def arrange(block):
        block = block.astype(jnp.float32)
        rows = [
            block[8 * z : 8 * z + 8, HEAD * g : HEAD * (g + 1)]
            for z in range(HEADS)
            for g in range(GROUP)
        ]
        return jnp.concatenate(rows, axis=0).astype(jnp.bfloat16)

    qbuf[0] = arrange(q_ref[...])
    acc[...] = jnp.zeros_like(acc)
    top[...] = jnp.full(top.shape, NEG, jnp.float32)

    pl.semaphore_wait(barrier, len(greeted))

    q_copy = remote(q_ref, qraw, s_q, r_q, across)
    q_copy.start()
    firsts = []
    for step in (1, 3, 2):
        chunk, half = step // 2, step % 2
        firsts.append(
            remote(k_ref, kbuf.at[0, chunk, pl.ds(half * KEYS, KEYS)],
                   s_first.at[step - 1], r_first.at[step - 1], first(step))
        )
        firsts.append(
            remote(vt_ref, vbuf.at[0, chunk, :, pl.ds(half * KEYS, KEYS)],
                   s_first.at[step + 2], r_first.at[step + 2], first(step))
        )
    for copy in firsts:
        copy.start()

    def scores(slot, chunk, part, queries):
        sbuf[part] = lax.dot_general(
            kbuf[slot, chunk], qbuf[queries], (((1,), (1,)), ((), ())),
            preferred_element_type=jnp.float32,
        )

    lead = lax.broadcasted_iota(jnp.int32, (SUF, COLS), 0)
    lane = lax.broadcasted_iota(jnp.int32, (SUF, COLS), 1)
    lead = lead - (lane // SUF * 8 + lane % 8)
    my_span = [span_ref[ctx], span_ref[place(1 - zh, u, w, c)]]

    def limit(slot, chunk, half, queries):
        whose = slot % 2
        batch = slot // 2
        core = c + whose - 2 * c * whose
        uu = u * (1 - whose) + w * whose
        ww = w * (1 - whose) + u * whose
        relative = chunk * 2 + half
        source = place(zh, (uu - relative + SIDE) % SIDE, (ww - batch + SIDE) % SIDE, core)
        return SUF * (my_span[queries] - span_ref[source])

    def absorb(slot, chunk, part, queries):
        pieces = []
        for half in range(2):
            base = half * KEYS
            pieces.append(sbuf[part, base : base + POOL])
            seen = lead <= limit(slot, chunk, half, queries)
            pieces.append(jnp.where(seen, sbuf[part, base + POOL : base + KEYS], NEG))
        peak = pieces[0].max(axis=0, keepdims=True)
        for piece in pieces[1:]:
            peak = jnp.maximum(peak, piece.max(axis=0, keepdims=True))
        old = top[queries, 0:1]
        new = jnp.maximum(old, peak * FACTOR)
        top[queries, 0:1] = new
        p = jnp.concatenate(
            [jnp.exp2(piece * FACTOR - new).astype(jnp.bfloat16) for piece in pieces], axis=0
        )
        acc[queries] = acc[queries] * jnp.exp2(old - new) + jnp.dot(
            vbuf[slot, chunk], p, preferred_element_type=jnp.float32
        )

    def line(slot, queries):
        scores(slot, 0, 0, queries)
        scores(slot, 1, 1, queries)
        absorb(slot, 0, 0, queries)
        absorb(slot, 1, 1, queries)

    def share(b, chunk):
        n = 2 * b + chunk
        return [
            remote(kbuf.at[2 * b, chunk], kbuf.at[2 * b + 1, chunk], s_core.at[n], r_core.at[n], partner),
            remote(vbuf.at[2 * b, chunk], vbuf.at[2 * b + 1, chunk], s_core.at[8 + n], r_core.at[8 + n], partner),
        ]

    def pass_on(source, target, chunk, n, who):
        return [
            remote(kbuf.at[2 * source, chunk], kbuf.at[2 * target, chunk], s_line.at[n], r_line.at[n], who),
            remote(vbuf.at[2 * source, chunk], vbuf.at[2 * target, chunk], s_line.at[6 + n], r_line.at[6 + n], who),
        ]

    def begin(copies):
        for copy in copies:
            copy.start()

    def arrived(copies):
        for copy in copies:
            copy.wait_recv()

    own_k.wait()
    own_v.wait()
    arrived(firsts)
    right = pass_on(0, 1, 0, 0, second(1)) + pass_on(0, 1, 1, 1, second(1))
    left = pass_on(0, 3, 0, 2, second(3)) + pass_on(0, 3, 1, 3, second(3))
    core = [share(b, chunk) for b in range(4) for chunk in range(2)]
    begin(right[:2] + left[2:] + right[2:] + left[:2])
    begin(core[0] + core[1])
    line(0, 0)
    arrived(core[0] + core[1])
    line(1, 0)
    turn_right = pass_on(1, 2, 0, 4, second(1))
    turn_left = pass_on(3, 2, 1, 5, second(3))
    arrived(right[:2])
    begin(turn_right)
    arrived(left[2:])
    begin(turn_left)
    arrived(right[2:])
    begin(core[2] + core[3])
    arrived(left[:2])
    begin(core[6] + core[7])
    line(2, 0)
    line(6, 0)
    arrived(core[2] + core[3])
    line(3, 0)
    arrived(turn_right + turn_left)
    begin(core[4] + core[5])
    arrived(core[6] + core[7])
    line(7, 0)
    line(4, 0)
    arrived(core[4] + core[5])
    line(5, 0)

    def finish(queries):
        total = acc[queries, HEAD : HEAD + 1]
        values = (acc[queries, 0:HEAD] * (1.0 / total)).T
        level = top[queries, 0:1] + jnp.log2(total)
        high = level.astype(jnp.bfloat16).astype(jnp.float32)
        middle = (level - high).astype(jnp.bfloat16).astype(jnp.float32)
        low = level - high - middle
        row = lax.broadcasted_iota(jnp.int32, (16, COLS), 0)
        stats = jnp.where(row == 0, high, jnp.where(row == 1, middle, jnp.where(row == 2, low, 0.0)))
        for z in range(HEADS):
            send[queries, z, 0:SUF] = values[SUF * z : SUF * (z + 1)].astype(jnp.bfloat16)
            near = z // 2 * HEAD
            send[queries, z, SUF:MSG] = stats[:, near : near + HEAD].astype(jnp.bfloat16)

    outs = {}
    for n, (flip, step) in enumerate(far):
        outs[flip, step] = remote(
            send.at[flip, (zl + step) % HEADS], land.at[flip, zl], s_out.at[n], r_out.at[n], column(flip, step)
        )
    finish(0)
    for step in (4, 3, 5, 2, 6, 1, 7):
        outs[0, step].start()
    land[0, zl] = send[0, zl]

    q_copy.wait_recv()
    qbuf[1] = arrange(qraw[...])

    def step_over(slot, carry):
        line(slot, 1)
        return carry

    lax.fori_loop(0, 8, step_over, 0)
    finish(1)
    for step in (4, 3, 5, 2, 6, 1, 7, 0):
        outs[1, step].start()

    for copy in outs.values():
        copy.wait_recv()

    def level_of(flip):
        rows = []
        for z in range(HEADS):
            tile = land[flip, z, SUF:MSG].astype(jnp.float32)
            rows.append(tile[0:1] + tile[1:2] + tile[2:3])
        return jnp.concatenate(rows, axis=0)

    near, other = level_of(0), level_of(1)
    peak = jnp.maximum(near, other)
    near, other = jnp.exp2(near - peak), jnp.exp2(other - peak)
    both = near + other
    weights[...] = jnp.concatenate([near / both, other / both], axis=0).T
    shares = weights[pl.ds(pl.multiple_of(zl % 2 * SUF, SUF), SUF)]
    for z in range(HEADS):
        o = land[0, z, 0:SUF].astype(jnp.float32) * shares[:, z : z + 1]
        o = o + land[1, z, 0:SUF].astype(jnp.float32) * shares[:, HEADS + z : HEADS + z + 1]
        row = jnp.concatenate([o[8 * g : 8 * g + 8] for g in range(GROUP)], axis=1)
        out_ref[:, z * GROUP * HEAD : (z + 1) * GROUP * HEAD] = row.astype(jnp.bfloat16)

    for copy in [q_copy] + firsts + right + left + turn_right + turn_left:
        copy.wait_send()
    for pair in core:
        for copy in pair:
            copy.wait_send()
    for copy in outs.values():
        copy.wait_send()


def per_device(queries, suffix_keys, suffix_values, prefix_keys, prefix_values, counts, span_order):
    ctx = lax.axis_index("ctx")
    count = lax.dynamic_slice(counts, (ctx,), (1,))[0]
    live = (jnp.arange(POOL) < count)[:, None]
    keys = jnp.concatenate([jnp.where(live, prefix_keys, prefix_keys[0:1]), suffix_keys])
    values = jnp.concatenate([jnp.where(live, prefix_values, 0), suffix_values])
    place = jnp.arange(KEYS)[None, :]
    ones = ((place < count) | (place >= POOL)) & (jnp.arange(VROWS - HEAD)[:, None] == 0)
    values = jnp.concatenate([values.T, ones.astype(jnp.bfloat16)])
    vmem = pl.BlockSpec(memory_space=pltpu.VMEM)
    dma = pltpu.SemaphoreType.DMA
    bf16, f32 = jnp.bfloat16, jnp.float32
    return pl.pallas_call(
        kernel,
        out_shape=jax.ShapeDtypeStruct((SUF // HEADS, HEADS * GROUP * HEAD), bf16),
        in_specs=[vmem, vmem, vmem, pl.BlockSpec(memory_space=pltpu.SMEM)],
        out_specs=vmem,
        scratch_shapes=[
            pltpu.VMEM((8, 2, WIDE, HEAD), bf16),
            pltpu.VMEM((8, 2, VROWS, WIDE), bf16),
            pltpu.VMEM((SUF, GROUP * HEAD), bf16),
            pltpu.VMEM((2, COLS, HEAD), bf16),
            pltpu.VMEM((2, WIDE, COLS), f32),
            pltpu.VMEM((2, VROWS, COLS), f32),
            pltpu.VMEM((2, 8, COLS), f32),
            pltpu.VMEM((2, HEADS, MSG, HEAD), bf16),
            pltpu.VMEM((2, HEADS, MSG, HEAD), bf16),
            pltpu.VMEM((HEAD, 2 * HEADS), f32),
            dma((6,)), dma((6,)), dma((12,)), dma((12,)), dma((16,)), dma((16,)),
            dma, dma, dma((15,)), dma((15,)), dma((2,)),
        ],
        compiler_params=pltpu.CompilerParams(
            collective_id=0, has_side_effects=True, vmem_limit_bytes=48 << 20
        ),
    )(queries, keys, values, span_order)


def solution(mesh):
    two = P("ctx", "head")
    return jax.shard_map(
        per_device,
        mesh=mesh,
        in_specs=(two, two, two, two, two, P(), P()),
        out_specs=P(("ctx", "head"), None),
        check_vma=False,
    )
```

```python
import math

import jax
import jax.numpy as jnp
from jax import lax
from jax.experimental import pallas as pl
from jax.experimental.pallas import tpu as pltpu
from jax.sharding import PartitionSpec as P

HEAD = 128
GROUP = 8
SUF = 64
POOL = 320
KEYS = POOL + SUF
WIDE = 2 * KEYS
VROWS = 144
COLS = SUF * GROUP
LIMIT = 63 << 20
SIDE = 4
HEADS = 8
NEG = -1e30
FACTOR = math.log2(math.e) / math.sqrt(HEAD)
MESH = pl.DeviceIdType.MESH


def kernel(
    q_ref, sk_ref, sv_ref, pk_ref, pv_ref, count_ref, span_ref, out_ref,
    kbuf, vbuf, qown, skv, pkv, qraw, qbuf, sbuf, acc, top, send, land, level_send, level_land, weights,
    s_first, r_first, s_line, r_line, s_core, r_core, s_q, r_q, s_out, r_out, s_own, reach,
):
    ctx, zl = lax.axis_index("ctx"), lax.axis_index("head")
    c = ctx % 2
    x = ctx // 2 % SIDE
    y = ctx // (2 * SIDE) % SIDE
    zh = ctx // (2 * SIDE * SIDE)
    u = y * (1 - c) + x * c
    w = x * (1 - c) + y * c

    def place(plane, first, second, core):
        row = first * (1 - core) + second * core
        col = second * (1 - core) + first * core
        return ((plane * SIDE + row) * SIDE + col) * 2 + core

    def first(step):
        return (place(zh, (u + step) % SIDE, w, c), zl)

    def second(step):
        return (place(zh, u, (w + step) % SIDE, c), zl)

    partner = (ctx + 1 - 2 * c, zl)
    across = (place(1 - zh, u, w, c), zl)

    def column(flip, step):
        plane = (zh + flip) % 2
        return (place(plane, u, w, c), (zl + step) % HEADS)

    far = [(flip, step) for flip in (1, 0) for step in (4, 3, 5, 2, 6, 1, 7, 0) if flip or step]

    barrier = pltpu.get_barrier_semaphore()

    def along(step):
        z = (zh * HEADS + zl + step) % (2 * HEADS)
        return (place(z // HEADS, u, w, c), z % HEADS)

    greeted = [first(1), first(2), first(3), second(1), second(3), partner, along(1), along(15)]
    for who in greeted:
        pl.semaphore_signal(barrier, inc=1, device_id=who, device_id_type=MESH)

    def remote(src, dst, s_sem, r_sem, who):
        return pltpu.make_async_remote_copy(
            src_ref=src, dst_ref=dst, send_sem=s_sem, recv_sem=r_sem,
            device_id=who, device_id_type=MESH,
        )

    loads = [
        pltpu.make_async_copy(source, target, s_own.at[n])
        for n, (source, target) in enumerate(
            [(pk_ref, pkv.at[0]), (sk_ref, skv.at[0]), (pv_ref, pkv.at[1]), (sv_ref, skv.at[1]), (q_ref, qown)]
        )
    ]
    for load in loads:
        load.start()

    def arrange(block):
        block = block.astype(jnp.float32)
        rows = [
            block[8 * z : 8 * z + 8, HEAD * g : HEAD * (g + 1)]
            for z in range(HEADS)
            for g in range(GROUP)
        ]
        return jnp.concatenate(rows, axis=0).astype(jnp.bfloat16)

    acc[...] = jnp.zeros_like(acc)
    top[...] = jnp.full(top.shape, NEG, jnp.float32)

    def batch_of(slot):
        rank = slot // 2
        return rank + rank // 2 - rank // 3 * 2

    def source_of(slot, chunk, half):
        whose = slot % 2
        core = c + whose - 2 * c * whose
        uu = u * (1 - whose) + w * whose
        ww = w * (1 - whose) + u * whose
        relative = chunk * 2 + half
        return place(zh, (uu - relative + SIDE) % SIDE, (ww - batch_of(slot) + SIDE) % SIDE, core)

    one_row = lax.broadcasted_iota(jnp.int32, (VROWS - HEAD, KEYS), 0)
    one_col = lax.broadcasted_iota(jnp.int32, (VROWS - HEAD, KEYS), 1)

    def ones_of(slot, carry):
        for chunk in range(2):
            for half in range(2):
                count = count_ref[source_of(slot, chunk, half)]
                row = jnp.where((one_row == 0) & ((one_col < count) | (one_col >= POOL)), 1.0, 0.0)
                vbuf[slot, chunk, HEAD:VROWS, half * KEYS : (half + 1) * KEYS] = row.astype(jnp.bfloat16)
        return carry

    lax.fori_loop(0, 8, ones_of, 0)

    for load in loads:
        load.wait()
    live = lax.broadcasted_iota(jnp.int32, (POOL, HEAD), 0) < count_ref[ctx]
    rows = pkv[0].astype(jnp.float32)
    kbuf[0, 0, 0:POOL] = jnp.where(live, rows, rows[0:1]).astype(jnp.bfloat16)
    kbuf[0, 0, POOL:KEYS] = skv[0]
    rows = jnp.where(live, pkv[1].astype(jnp.float32), 0.0)
    rows = jnp.concatenate([rows, skv[1].astype(jnp.float32)], axis=0)
    vbuf[0, 0, 0:HEAD, 0:KEYS] = rows.T.astype(jnp.bfloat16)

    pl.semaphore_wait(barrier, len(greeted))

    def keys_at(slot, piece):
        return kbuf.at[slot, piece // 2, pl.ds(piece % 2 * KEYS, KEYS)]

    def values_at(slot, piece):
        return vbuf.at[slot, piece // 2, pl.ds(0, HEAD), pl.ds(piece % 2 * KEYS, KEYS)]

    def forward(source, target, piece, n, s_sem, r_sem, who):
        begins = 0 if s_sem is s_first else piece
        return [
            remote(keys_at(source, begins), keys_at(target, piece), s_sem.at[2 * n], r_sem.at[2 * n], who),
            remote(values_at(source, begins), values_at(target, piece), s_sem.at[2 * n + 1], r_sem.at[2 * n + 1], who),
        ]

    def begin(*groups):
        for group in groups:
            for copy in group:
                copy.start()

    def arrived(*groups):
        for group in groups:
            for copy in group:
                copy.wait_recv()

    ahead = {r: forward(0, 0, r, r - 1, s_first, r_first, first(r)) for r in (1, 3, 2)}
    right = [forward(0, 2, r, r, s_line, r_line, second(1)) for r in range(4)]
    left = [forward(0, 4, r, 4 + r, s_line, r_line, second(3)) for r in range(4)]
    turn_right = [forward(2, 6, r, 8 + r, s_line, r_line, second(1)) for r in (0, 1)]
    turn_left = [forward(4, 6, r, 8 + r, s_line, r_line, second(3)) for r in (2, 3)]
    q_copy = remote(qown, qraw, s_q, r_q, across)
    begin(ahead[1], ahead[3], right[0], left[0], ahead[2])
    for n in range(3):
        for step in (1 << n, 16 - (1 << n)):
            pl.semaphore_signal(reach.at[n], inc=1, device_id=along(step), device_id_type=MESH)
        pl.semaphore_wait(reach.at[n], 2)
    q_copy.start()
    qbuf[0] = arrange(qown[...])

    def scores(slot, chunk, part, queries):
        sbuf[part] = lax.dot_general(
            kbuf[slot, chunk], qbuf[queries], (((1,), (1,)), ((), ())),
            preferred_element_type=jnp.float32,
        )

    lead = lax.broadcasted_iota(jnp.int32, (SUF, COLS), 0)
    lane = lax.broadcasted_iota(jnp.int32, (SUF, COLS), 1)
    lead = lead - (lane // SUF * 8 + lane % 8)
    my_span = [span_ref[ctx], span_ref[place(1 - zh, u, w, c)]]

    def limit(slot, chunk, half, queries):
        return SUF * (my_span[queries] - span_ref[source_of(slot, chunk, half)])

    def absorb(slot, chunk, part, queries):
        pieces = []
        for half in range(2):
            base = half * KEYS
            pieces.append(sbuf[part, base : base + POOL])
            seen = lead <= limit(slot, chunk, half, queries)
            pieces.append(jnp.where(seen, sbuf[part, base + POOL : base + KEYS], NEG))
        peak = pieces[0].max(axis=0, keepdims=True)
        for piece in pieces[1:]:
            peak = jnp.maximum(peak, piece.max(axis=0, keepdims=True))
        old = top[queries, 0:1]
        new = jnp.maximum(old, peak * FACTOR)
        top[queries, 0:1] = new
        p = jnp.concatenate(
            [jnp.exp2(piece * FACTOR - new).astype(jnp.bfloat16) for piece in pieces], axis=0
        )
        acc[queries] = acc[queries] * jnp.exp2(old - new) + jnp.dot(
            vbuf[slot, chunk], p, preferred_element_type=jnp.float32
        )

    def sweep(count, pick, queries):
        scores(*pick(0, 0), 0, queries)

        def pair(i, carry):
            later = jnp.minimum(i + 1, count - 1)
            scores(*pick(i, 1), 1, queries)
            absorb(*pick(i, 0), 0, queries)
            scores(*pick(later, 0), 0, queries)
            absorb(*pick(i, 1), 1, queries)
            return carry

        lax.fori_loop(0, count, pair, 0)

    def share(r, chunk):
        n = 2 * r + chunk
        rows = pl.ds(0, HEAD)
        return [
            remote(kbuf.at[2 * r, chunk], kbuf.at[2 * r + 1, chunk], s_core.at[n], r_core.at[n], partner),
            remote(vbuf.at[2 * r, chunk, rows], vbuf.at[2 * r + 1, chunk, rows], s_core.at[8 + n], r_core.at[8 + n], partner),
        ]

    core = [[share(r, chunk) for chunk in range(2)] for r in range(4)]
    arrived(ahead[1])
    begin(right[1], left[1], core[0][0])
    arrived(right[0])
    begin(turn_right[0])
    arrived(ahead[3])
    begin(right[3], left[3])
    arrived(ahead[2])
    begin(right[2], left[2], core[0][1])
    sweep(1, lambda i, j: (0, j), 0)
    arrived(*core[0])
    sweep(1, lambda i, j: (1, j), 0)
    arrived(right[1])
    begin(turn_right[1], core[1][0])
    arrived(left[3])
    begin(turn_left[1])
    arrived(left[0], left[1])
    begin(core[2][0])
    sweep(1, lambda i, j: (2 + 2 * j, 0), 0)
    arrived(right[3], right[2])
    begin(core[1][1])
    arrived(left[2])
    begin(turn_left[0], core[2][1])
    arrived(core[1][0], core[2][0])
    sweep(1, lambda i, j: (3 + 2 * j, 0), 0)
    sweep(1, lambda i, j: (2 + 2 * j, 1), 0)
    arrived(core[1][1], core[2][1])
    sweep(1, lambda i, j: (3 + 2 * j, 1), 0)
    q_copy.wait_recv()
    qbuf[1] = arrange(qraw[...])
    sweep(3, lambda i, j: (i, j), 1)
    arrived(*turn_right)
    begin(core[3][0])
    arrived(*turn_left)
    begin(core[3][1])
    sweep(3, lambda i, j: (3 + i, j), 1)
    arrived(*core[3])
    sweep(2, lambda i, j: (6 + i, j), 1)

    def finish(queries):
        total = acc[queries, HEAD : HEAD + 1]
        values = (acc[queries, 0:HEAD] * (1.0 / total)).T
        level = top[queries, 0:1] + jnp.log2(total)
        for z in range(HEADS):
            send[queries, z] = values[SUF * z : SUF * (z + 1)].astype(jnp.bfloat16)
            near = z // 2 * HEAD
            level_send[queries, z, 0:1] = level[:, near : near + HEAD]

    outs = {}
    for n, (flip, step) in enumerate(far):
        who, to = column(flip, step), (zl + step) % HEADS
        row = pl.ds(0, 1)
        outs[flip, step] = [
            remote(level_send.at[flip, to, row], level_land.at[flip, zl, row], s_out.at[n], r_out.at[n], who),
            remote(send.at[flip, to], land.at[flip, zl], s_out.at[15 + n], r_out.at[15 + n], who),
        ]
    finish(1)
    for step in (4, 3, 5, 2, 6, 1, 7, 0):
        begin(outs[1, step])
    sweep(2, lambda i, j: (6 + i, j), 0)
    finish(0)
    for step in (4, 3, 5, 2, 6, 1, 7):
        begin(outs[0, step])
    land[0, zl] = send[0, zl]
    level_land[0, zl, 0:1] = level_send[0, zl, 0:1]

    arrived(*outs.values())

    def level_of(flip):
        return jnp.concatenate([level_land[flip, z, 0:1] for z in range(HEADS)], axis=0)

    near, other = level_of(0), level_of(1)
    peak = jnp.maximum(near, other)
    near, other = jnp.exp2(near - peak), jnp.exp2(other - peak)
    both = near + other
    weights[...] = jnp.concatenate([near / both, other / both], axis=0).T
    shares = weights[pl.ds(pl.multiple_of(zl % 2 * SUF, SUF), SUF)]
    for z in range(HEADS):
        o = land[0, z].astype(jnp.float32) * shares[:, z : z + 1]
        o = o + land[1, z].astype(jnp.float32) * shares[:, HEADS + z : HEADS + z + 1]
        row = jnp.concatenate([o[8 * g : 8 * g + 8] for g in range(GROUP)], axis=1)
        out_ref[:, z * GROUP * HEAD : (z + 1) * GROUP * HEAD] = row.astype(jnp.bfloat16)

    q_copy.wait_send()
    for group in [*ahead.values(), *right, *left, *turn_right, *turn_left, *core[0], *core[1], *core[2], *core[3], *outs.values()]:
        for copy in group:
            copy.wait_send()


def per_device(queries, suffix_keys, suffix_values, prefix_keys, prefix_values, counts, span_order):
    smem = pl.BlockSpec(memory_space=pltpu.SMEM)
    stays = pl.BlockSpec(memory_space=pltpu.HBM)
    vmem = pl.BlockSpec(memory_space=pltpu.VMEM)
    dma = pltpu.SemaphoreType.DMA
    bf16, f32 = jnp.bfloat16, jnp.float32
    return pl.pallas_call(
        kernel,
        out_shape=jax.ShapeDtypeStruct((SUF // HEADS, HEADS * GROUP * HEAD), bf16),
        in_specs=[stays] * 5 + [smem] * 2,
        out_specs=vmem,
        scratch_shapes=[
            pltpu.VMEM((8, 2, WIDE, HEAD), bf16),
            pltpu.VMEM((8, 2, VROWS, WIDE), bf16),
            pltpu.VMEM((SUF, GROUP * HEAD), bf16),
            pltpu.VMEM((2, SUF, HEAD), bf16),
            pltpu.VMEM((2, POOL, HEAD), bf16),
            pltpu.VMEM((SUF, GROUP * HEAD), bf16),
            pltpu.VMEM((2, COLS, HEAD), bf16),
            pltpu.VMEM((2, WIDE, COLS), f32),
            pltpu.VMEM((2, VROWS, COLS), f32),
            pltpu.VMEM((2, 8, COLS), f32),
            pltpu.VMEM((2, HEADS, SUF, HEAD), bf16),
            pltpu.VMEM((2, HEADS, SUF, HEAD), bf16),
            pltpu.VMEM((2, HEADS, 8, HEAD), f32),
            pltpu.VMEM((2, HEADS, 8, HEAD), f32),
            pltpu.VMEM((HEAD, 2 * HEADS), f32),
            dma((6,)), dma((6,)), dma((24,)), dma((24,)), dma((16,)), dma((16,)),
            dma, dma, dma((30,)), dma((30,)), dma((5,)), pltpu.SemaphoreType.REGULAR((3,)),
        ],
        compiler_params=pltpu.CompilerParams(
            collective_id=0, has_side_effects=True, vmem_limit_bytes=LIMIT
        ),
    )(queries, suffix_keys, suffix_values, prefix_keys, prefix_values, counts, span_order)


def solution(mesh):
    two = P("ctx", "head")
    return jax.shard_map(
        per_device,
        mesh=mesh,
        in_specs=(two, two, two, two, two, P(), P()),
        out_specs=P(("ctx", "head"), None),
        check_vma=False,
    )
```

```python
import math

import jax
import jax.numpy as jnp
from jax import lax
from jax.experimental import pallas as pl
from jax.experimental.pallas import tpu as pltpu
from jax.sharding import PartitionSpec as P

HEAD = 128
GROUP = 8
SUF = 64
POOL = 320
KEYS = POOL + SUF
WIDE = 2 * KEYS
VROWS = 144
COLS = SUF * GROUP
LIMIT = 63 << 20
SIDE = 4
HEADS = 8
NEG = -1e30
FACTOR = math.log2(math.e) / math.sqrt(HEAD)
MESH = pl.DeviceIdType.MESH


def kernel(
    q_ref, sk_ref, sv_ref, pk_ref, pv_ref, count_ref, span_ref, out_ref,
    kbuf, vbuf, qown, skv, pkv, qraw, qbuf, sbuf, acc, top, send, land, level_send, level_land, flat, share_of, weights,
    s_first, r_first, s_line, r_line, s_core, r_core, s_q, r_q, s_out, r_out, s_own, reach,
):
    ctx, zl = lax.axis_index("ctx"), lax.axis_index("head")
    c = ctx % 2
    x = ctx // 2 % SIDE
    y = ctx // (2 * SIDE) % SIDE
    zh = ctx // (2 * SIDE * SIDE)
    u = y * (1 - c) + x * c
    w = x * (1 - c) + y * c

    def place(plane, first, second, core):
        row = first * (1 - core) + second * core
        col = second * (1 - core) + first * core
        return ((plane * SIDE + row) * SIDE + col) * 2 + core

    def first(step):
        return (place(zh, (u + step) % SIDE, w, c), zl)

    def second(step):
        return (place(zh, u, (w + step) % SIDE, c), zl)

    partner = (ctx + 1 - 2 * c, zl)
    across = (place(1 - zh, u, w, c), zl)

    def column(flip, step):
        plane = (zh + flip) % 2
        return (place(plane, u, w, c), (zl + step) % HEADS)

    far = [(flip, step) for flip in (1, 0) for step in (4, 3, 5, 2, 6, 1, 7, 0) if flip or step]

    barrier = pltpu.get_barrier_semaphore()

    def along(step):
        z = (zh * HEADS + zl + step) % (2 * HEADS)
        return (place(z // HEADS, u, w, c), z % HEADS)

    greeted = [first(1), first(2), first(3), second(1), second(3), partner]
    greeted += [along(step) for k in (1, 2, 3, 4) for step in (k, 16 - k)]
    for who in greeted:
        pl.semaphore_signal(barrier, inc=1, device_id=who, device_id_type=MESH)

    def remote(src, dst, s_sem, r_sem, who):
        return pltpu.make_async_remote_copy(
            src_ref=src, dst_ref=dst, send_sem=s_sem, recv_sem=r_sem,
            device_id=who, device_id_type=MESH,
        )

    loads = [
        pltpu.make_async_copy(source, target, s_own.at[n])
        for n, (source, target) in enumerate(
            [(pk_ref, pkv.at[0]), (sk_ref, skv.at[0]), (pv_ref, pkv.at[1]), (sv_ref, skv.at[1]), (q_ref, qown)]
        )
    ]
    for load in loads:
        load.start()

    def arrange(block):
        block = block.astype(jnp.float32)
        rows = [
            block[8 * z : 8 * z + 8, HEAD * g : HEAD * (g + 1)]
            for z in range(HEADS)
            for g in range(GROUP)
        ]
        return jnp.concatenate(rows, axis=0).astype(jnp.bfloat16)

    acc[...] = jnp.zeros_like(acc)
    top[...] = jnp.full(top.shape, NEG, jnp.float32)

    def batch_of(slot):
        rank = slot // 2
        return rank + rank // 2 - rank // 3 * 2

    def source_of(slot, chunk, half):
        whose = slot % 2
        core = c + whose - 2 * c * whose
        uu = u * (1 - whose) + w * whose
        ww = w * (1 - whose) + u * whose
        relative = chunk * 2 + half
        return place(zh, (uu - relative + SIDE) % SIDE, (ww - batch_of(slot) + SIDE) % SIDE, core)

    one_row = lax.broadcasted_iota(jnp.int32, (VROWS - HEAD, KEYS), 0)
    one_col = lax.broadcasted_iota(jnp.int32, (VROWS - HEAD, KEYS), 1)

    def ones_of(slot, carry):
        for chunk in range(2):
            for half in range(2):
                count = count_ref[source_of(slot, chunk, half)]
                row = jnp.where((one_row == 0) & ((one_col < count) | (one_col >= POOL)), 1.0, 0.0)
                vbuf[slot, chunk, HEAD:VROWS, half * KEYS : (half + 1) * KEYS] = row.astype(jnp.bfloat16)
        return carry

    lax.fori_loop(0, 8, ones_of, 0)

    for load in loads:
        load.wait()
    live = lax.broadcasted_iota(jnp.int32, (POOL, HEAD), 0) < count_ref[ctx]
    rows = pkv[0].astype(jnp.float32)
    kbuf[0, 0, 0:POOL] = jnp.where(live, rows, rows[0:1]).astype(jnp.bfloat16)
    kbuf[0, 0, POOL:KEYS] = skv[0]
    rows = jnp.where(live, pkv[1].astype(jnp.float32), 0.0)
    rows = jnp.concatenate([rows, skv[1].astype(jnp.float32)], axis=0)
    vbuf[0, 0, 0:HEAD, 0:KEYS] = rows.T.astype(jnp.bfloat16)

    pl.semaphore_wait(barrier, len(greeted))

    def keys_at(slot, piece):
        return kbuf.at[slot, piece // 2, pl.ds(piece % 2 * KEYS, KEYS)]

    def values_at(slot, piece):
        return vbuf.at[slot, piece // 2, pl.ds(0, HEAD), pl.ds(piece % 2 * KEYS, KEYS)]

    def forward(source, target, piece, n, s_sem, r_sem, who):
        begins = 0 if s_sem is s_first else piece
        return [
            remote(keys_at(source, begins), keys_at(target, piece), s_sem.at[2 * n], r_sem.at[2 * n], who),
            remote(values_at(source, begins), values_at(target, piece), s_sem.at[2 * n + 1], r_sem.at[2 * n + 1], who),
        ]

    def begin(*groups):
        for group in groups:
            for copy in group:
                copy.start()

    def arrived(*groups):
        for group in groups:
            for copy in group:
                copy.wait_recv()

    ahead = {r: forward(0, 0, r, r - 1, s_first, r_first, first(r)) for r in (1, 3, 2)}
    right = [forward(0, 2, r, r, s_line, r_line, second(1)) for r in range(4)]
    left = [forward(0, 4, r, 4 + r, s_line, r_line, second(3)) for r in range(4)]
    turn_right = forward(2, 6, 0, 8, s_line, r_line, second(1))
    turn_left = forward(4, 6, 3, 11, s_line, r_line, second(3))
    turn_keys = {r: [forward(2, 6, r, 8 + r, s_line, r_line, second(1))[0]] for r in (1, 2)}
    turn_values = {r: [forward(4, 6, r, 8 + r, s_line, r_line, second(3))[1]] for r in (1, 2)}
    q_copy = remote(qown, qraw, s_q, r_q, across)
    begin(ahead[1], ahead[3], right[0], left[0], ahead[2])
    for n, k in enumerate((4,)):
        for step in (k, 16 - k):
            pl.semaphore_signal(reach.at[n], inc=1, device_id=along(step), device_id_type=MESH)
        pl.semaphore_wait(reach.at[n], 2)
    q_copy.start()
    qbuf[0] = arrange(qown[...])

    def scores(slot, chunk, part, queries):
        sbuf[part] = lax.dot_general(
            kbuf[slot, chunk], qbuf[queries], (((1,), (1,)), ((), ())),
            preferred_element_type=jnp.float32,
        )

    lead = lax.broadcasted_iota(jnp.int32, (SUF, COLS), 0)
    lane = lax.broadcasted_iota(jnp.int32, (SUF, COLS), 1)
    lead = lead - (lane // SUF * 8 + lane % 8)
    my_span = [span_ref[ctx], span_ref[place(1 - zh, u, w, c)]]

    def limit(slot, chunk, half, queries):
        return SUF * (my_span[queries] - span_ref[source_of(slot, chunk, half)])

    def absorb(slot, chunk, part, queries):
        pieces = []
        for half in range(2):
            base = half * KEYS
            pieces.append(sbuf[part, base : base + POOL])
            seen = lead <= limit(slot, chunk, half, queries)
            pieces.append(jnp.where(seen, sbuf[part, base + POOL : base + KEYS], NEG))
        peak = pieces[0].max(axis=0, keepdims=True)
        for piece in pieces[1:]:
            peak = jnp.maximum(peak, piece.max(axis=0, keepdims=True))
        old = top[queries, 0:1]
        new = jnp.maximum(old, peak * FACTOR)
        top[queries, 0:1] = new
        p = jnp.concatenate(
            [jnp.exp2(piece * FACTOR - new).astype(jnp.bfloat16) for piece in pieces], axis=0
        )
        acc[queries] = acc[queries] * jnp.exp2(old - new) + jnp.dot(
            vbuf[slot, chunk], p, preferred_element_type=jnp.float32
        )

    def sweep(count, pick, queries):
        scores(*pick(0, 0), 0, queries)

        def pair(i, carry):
            later = jnp.minimum(i + 1, count - 1)
            scores(*pick(i, 1), 1, queries)
            absorb(*pick(i, 0), 0, queries)
            scores(*pick(later, 0), 0, queries)
            absorb(*pick(i, 1), 1, queries)
            return carry

        lax.fori_loop(0, count, pair, 0)

    def share(r, chunk):
        n = 2 * r + chunk
        rows = pl.ds(0, HEAD)
        return [
            remote(kbuf.at[2 * r, chunk], kbuf.at[2 * r + 1, chunk], s_core.at[n], r_core.at[n], partner),
            remote(vbuf.at[2 * r, chunk, rows], vbuf.at[2 * r + 1, chunk, rows], s_core.at[8 + n], r_core.at[8 + n], partner),
        ]

    core = [[share(r, chunk) for chunk in range(2)] for r in range(4)]
    def hop(source, *targets):
        for n in range(2):
            arrived(source[n : n + 1])
            begin(*[target[n : n + 1] for target in targets])

    hop(ahead[1], right[1], left[1])
    begin(core[0][0])
    hop(ahead[3], right[3], left[3])
    hop(ahead[2], right[2], left[2])
    begin(core[0][1])
    hop(right[0], turn_right)
    arrived(core[0][0])
    sweep(1, lambda i, j: (j, 0), 0)
    arrived(right[1][:1])
    begin(turn_keys[1])
    arrived(left[1][1:])
    begin(turn_values[1])
    hop(left[3], turn_left)
    arrived(right[1][1:])
    begin(core[1][0])
    arrived(left[0], left[1][:1])
    begin(core[2][0])
    arrived(core[0][1])
    sweep(1, lambda i, j: (j, 1), 0)
    sweep(1, lambda i, j: (2 + 2 * j, 0), 0)
    arrived(right[2][:1])
    begin(turn_keys[2])
    arrived(left[2][1:])
    begin(turn_values[2])
    arrived(left[2][:1])
    begin(core[2][1])
    arrived(right[2][1:], right[3])
    begin(core[1][1])
    arrived(core[1][0], core[2][0])
    sweep(1, lambda i, j: (3 + 2 * j, 0), 0)
    q_copy.wait_recv()
    qbuf[1] = arrange(qraw[...])
    sweep(2, lambda i, j: (i, j), 1)
    arrived(turn_right, turn_keys[1], turn_values[1])
    begin(core[3][0])
    arrived(core[1][1], core[2][1])
    sweep(2, lambda i, j: (2 + i, j), 1)
    arrived(turn_left, turn_keys[2], turn_values[2])
    begin(core[3][1])
    sweep(3, lambda i, j: (4 + i, j), 1)
    arrived(*core[3])
    sweep(1, lambda i, j: (7, j), 1)

    def finish(queries, order):
        total = acc[queries, HEAD : HEAD + 1]
        level = top[queries, 0:1] + jnp.log2(total)
        for z in range(HEADS):
            near = z // 2 * HEAD
            level_send[queries, z, 0:1] = level[:, near : near + HEAD]
        for step in order:
            begin(outs[queries, step][:1])
        flat[...] = (acc[queries, 0:HEAD] * (1.0 / total)).T
        for step in order:
            to = (zl + step) % HEADS
            send[queries, to] = flat[pl.ds(pl.multiple_of(to * SUF, SUF), SUF)].astype(jnp.bfloat16)
            begin(outs[queries, step][1:])

    outs = {}
    for n, (flip, step) in enumerate(far):
        who, to = column(flip, step), (zl + step) % HEADS
        row = pl.ds(0, 1)
        outs[flip, step] = [
            remote(level_send.at[flip, to, row], level_land.at[flip, zl, row], s_out.at[n], r_out.at[n], who),
            remote(send.at[flip, to], land.at[flip, zl], s_out.at[15 + n], r_out.at[15 + n], who),
        ]
    finish(1, (4, 3, 5, 2, 6, 1, 7, 0))
    sweep(2, lambda i, j: (2 + 2 * i + j, 1), 0)
    sweep(2, lambda i, j: (6 + i, j), 0)
    finish(0, (4, 3, 5, 2, 6, 1, 7))
    send[0, zl] = flat[pl.ds(pl.multiple_of(zl * SUF, SUF), SUF)].astype(jnp.bfloat16)
    land[0, zl] = send[0, zl]
    level_land[0, zl, 0:1] = level_send[0, zl, 0:1]
    arrived(*[copies[:1] for copies in outs.values()])

    def level_of(flip):
        return jnp.concatenate([level_land[flip, z, 0:1] for z in range(HEADS)], axis=0)

    near, other = level_of(0), level_of(1)
    peak = jnp.maximum(near, other)
    near, other = jnp.exp2(near - peak), jnp.exp2(other - peak)
    both = near + other
    weights[...] = jnp.concatenate([near / both, other / both], axis=0).T
    shares = weights[pl.ds(pl.multiple_of(zl % 2 * SUF, SUF), SUF)]
    for n in range(2 * HEADS):
        share_of[n] = jnp.broadcast_to(shares[:, n : n + 1], (SUF, HEAD))
    for step in (0, 4, 3, 5, 2, 6, 1, 7):
        z = (zl + HEADS - step) % HEADS
        arrived(outs[1, step][1:])
        if step:
            arrived(outs[0, step][1:])
        o = land[0, z].astype(jnp.float32) * share_of[z]
        o = o + land[1, z].astype(jnp.float32) * share_of[HEADS + z]
        row = jnp.concatenate([o[8 * g : 8 * g + 8] for g in range(GROUP)], axis=1)
        start = pl.multiple_of(z * GROUP * HEAD, GROUP * HEAD)
        out_ref[:, pl.ds(start, GROUP * HEAD)] = row.astype(jnp.bfloat16)

    q_copy.wait_send()
    for group in [*ahead.values(), *right, *left, turn_right, turn_left, *turn_keys.values(), *turn_values.values(), *core[0], *core[1], *core[2], *core[3], *outs.values()]:
        for copy in group:
            copy.wait_send()


def per_device(queries, suffix_keys, suffix_values, prefix_keys, prefix_values, counts, span_order):
    smem = pl.BlockSpec(memory_space=pltpu.SMEM)
    stays = pl.BlockSpec(memory_space=pltpu.HBM)
    vmem = pl.BlockSpec(memory_space=pltpu.VMEM)
    dma = pltpu.SemaphoreType.DMA
    bf16, f32 = jnp.bfloat16, jnp.float32
    return pl.pallas_call(
        kernel,
        out_shape=jax.ShapeDtypeStruct((SUF // HEADS, HEADS * GROUP * HEAD), bf16),
        in_specs=[stays] * 5 + [smem] * 2,
        out_specs=vmem,
        scratch_shapes=[
            pltpu.VMEM((8, 2, WIDE, HEAD), bf16),
            pltpu.VMEM((8, 2, VROWS, WIDE), bf16),
            pltpu.VMEM((SUF, GROUP * HEAD), bf16),
            pltpu.VMEM((2, SUF, HEAD), bf16),
            pltpu.VMEM((2, POOL, HEAD), bf16),
            pltpu.VMEM((SUF, GROUP * HEAD), bf16),
            pltpu.VMEM((2, COLS, HEAD), bf16),
            pltpu.VMEM((2, WIDE, COLS), f32),
            pltpu.VMEM((2, VROWS, COLS), f32),
            pltpu.VMEM((2, 8, COLS), f32),
            pltpu.VMEM((2, HEADS, SUF, HEAD), bf16),
            pltpu.VMEM((2, HEADS, SUF, HEAD), bf16),
            pltpu.VMEM((2, HEADS, 8, HEAD), f32),
            pltpu.VMEM((2, HEADS, 8, HEAD), f32),
            pltpu.VMEM((COLS, HEAD), f32),
            pltpu.VMEM((2 * HEADS, SUF, HEAD), f32),
            pltpu.VMEM((HEAD, 2 * HEADS), f32),
            dma((6,)), dma((6,)), dma((24,)), dma((24,)), dma((16,)), dma((16,)),
            dma, dma, dma((30,)), dma((30,)), dma((5,)), pltpu.SemaphoreType.REGULAR((1,)),
        ],
        compiler_params=pltpu.CompilerParams(
            collective_id=0, has_side_effects=True, vmem_limit_bytes=LIMIT
        ),
    )(queries, suffix_keys, suffix_values, prefix_keys, prefix_values, counts, span_order)


def solution(mesh):
    two = P("ctx", "head")
    return jax.shard_map(
        per_device,
        mesh=mesh,
        in_specs=(two, two, two, two, two, P(), P()),
        out_specs=P(("ctx", "head"), None),
        check_vma=False,
    )
```

```python
import math

import jax
import jax.numpy as jnp
from jax import lax
from jax.experimental import pallas as pl
from jax.experimental.pallas import tpu as pltpu
from jax.sharding import PartitionSpec as P

HEAD = 128
GROUP = 8
SUF = 64
POOL = 320
KEYS = POOL + SUF
WIDE = 2 * KEYS
VROWS = 144
COLS = SUF * GROUP
LIMIT = 63 << 20
SIDE = 4
HEADS = 8
NEG = -1e30
FACTOR = math.log2(math.e) / math.sqrt(HEAD)
MESH = pl.DeviceIdType.MESH


def kernel(
    q_ref, sk_ref, sv_ref, pk_ref, pv_ref, count_ref, span_ref, out_ref,
    kbuf, vbuf, qown, skv, pkv, qraw, qbuf, sbuf, acc, top, send, land, level_send, level_land, flat, share_of, weights,
    s_first, r_first, s_line, r_line, s_core, r_core, s_q, r_q, s_out, r_out, s_own, reach,
):
    ctx, zl = lax.axis_index("ctx"), lax.axis_index("head")
    c = ctx % 2
    x = ctx // 2 % SIDE
    y = ctx // (2 * SIDE) % SIDE
    zh = ctx // (2 * SIDE * SIDE)
    u = y * (1 - c) + x * c
    w = x * (1 - c) + y * c

    def place(plane, first, second, core):
        row = first * (1 - core) + second * core
        col = second * (1 - core) + first * core
        return ((plane * SIDE + row) * SIDE + col) * 2 + core

    def first(step):
        return (place(zh, (u + step) % SIDE, w, c), zl)

    def second(step):
        return (place(zh, u, (w + step) % SIDE, c), zl)

    partner = (ctx + 1 - 2 * c, zl)
    across = (place(1 - zh, u, w, c), zl)

    def column(flip, step):
        plane = (zh + flip) % 2
        return (place(plane, u, w, c), (zl + step) % HEADS)

    far = [(flip, step) for flip in (1, 0) for step in (4, 3, 5, 2, 6, 1, 7, 0) if flip or step]

    barrier = pltpu.get_barrier_semaphore()

    def along(step):
        z = (zh * HEADS + zl + step) % (2 * HEADS)
        return (place(z // HEADS, u, w, c), z % HEADS)

    greeted = [first(1), first(2), first(3), second(1), second(3), partner]
    greeted += [along(step) for k in (1, 2, 3, 4) for step in (k, 16 - k)]
    for who in greeted:
        pl.semaphore_signal(barrier, inc=1, device_id=who, device_id_type=MESH)

    def remote(src, dst, s_sem, r_sem, who):
        return pltpu.make_async_remote_copy(
            src_ref=src, dst_ref=dst, send_sem=s_sem, recv_sem=r_sem,
            device_id=who, device_id_type=MESH,
        )

    loads = [
        pltpu.make_async_copy(source, target, s_own.at[n])
        for n, (source, target) in enumerate(
            [(pk_ref, pkv.at[0]), (sk_ref, skv.at[0]), (pv_ref, pkv.at[1]), (sv_ref, skv.at[1]), (q_ref, qown)]
        )
    ]
    for load in loads:
        load.start()

    def arrange(block):
        block = block.astype(jnp.float32)
        rows = [
            block[8 * z : 8 * z + 8, HEAD * g : HEAD * (g + 1)]
            for z in range(HEADS)
            for g in range(GROUP)
        ]
        return jnp.concatenate(rows, axis=0).astype(jnp.bfloat16)

    acc[...] = jnp.zeros_like(acc)
    top[...] = jnp.full(top.shape, NEG, jnp.float32)

    def batch_of(slot):
        rank = slot // 2
        return rank + rank // 2 - rank // 3 * 2

    def source_of(slot, chunk, half):
        whose = slot % 2
        core = c + whose - 2 * c * whose
        uu = u * (1 - whose) + w * whose
        ww = w * (1 - whose) + u * whose
        relative = chunk * 2 + half
        return place(zh, (uu - relative + SIDE) % SIDE, (ww - batch_of(slot) + SIDE) % SIDE, core)

    one_row = lax.broadcasted_iota(jnp.int32, (VROWS - HEAD, KEYS), 0)
    one_col = lax.broadcasted_iota(jnp.int32, (VROWS - HEAD, KEYS), 1)

    def ones_of(slot, carry):
        for chunk in range(2):
            for half in range(2):
                count = count_ref[source_of(slot, chunk, half)]
                row = jnp.where((one_row == 0) & ((one_col < count) | (one_col >= POOL)), 1.0, 0.0)
                vbuf[slot, chunk, HEAD:VROWS, half * KEYS : (half + 1) * KEYS] = row.astype(jnp.bfloat16)
        return carry

    lax.fori_loop(0, 8, ones_of, 0)

    for load in loads:
        load.wait()
    live = lax.broadcasted_iota(jnp.int32, (POOL, HEAD), 0) < count_ref[ctx]
    rows = pkv[0].astype(jnp.float32)
    kbuf[0, 0, 0:POOL] = jnp.where(live, rows, rows[0:1]).astype(jnp.bfloat16)
    kbuf[0, 0, POOL:KEYS] = skv[0]
    rows = jnp.where(live, pkv[1].astype(jnp.float32), 0.0)
    rows = jnp.concatenate([rows, skv[1].astype(jnp.float32)], axis=0)
    vbuf[0, 0, 0:HEAD, 0:KEYS] = rows.T.astype(jnp.bfloat16)

    pl.semaphore_wait(barrier, len(greeted))
    for step in (4, 12):
        pl.semaphore_signal(reach.at[0], inc=1, device_id=along(step), device_id_type=MESH)

    def keys_at(slot, piece):
        return kbuf.at[slot, piece // 2, pl.ds(piece % 2 * KEYS, KEYS)]

    def values_at(slot, piece):
        return vbuf.at[slot, piece // 2, pl.ds(0, HEAD), pl.ds(piece % 2 * KEYS, KEYS)]

    def forward(source, target, piece, n, s_sem, r_sem, who):
        begins = 0 if s_sem is s_first else piece
        return [
            remote(keys_at(source, begins), keys_at(target, piece), s_sem.at[2 * n], r_sem.at[2 * n], who),
            remote(values_at(source, begins), values_at(target, piece), s_sem.at[2 * n + 1], r_sem.at[2 * n + 1], who),
        ]

    def begin(*groups):
        for group in groups:
            for copy in group:
                copy.start()

    def arrived(*groups):
        for group in groups:
            for copy in group:
                copy.wait_recv()

    ahead = {r: forward(0, 0, r, r - 1, s_first, r_first, first(r)) for r in (1, 3, 2)}
    right = [forward(0, 2, r, r, s_line, r_line, second(1)) for r in range(4)]
    left = [forward(0, 4, r, 4 + r, s_line, r_line, second(3)) for r in range(4)]
    turn_right = forward(2, 6, 0, 8, s_line, r_line, second(1))
    turn_left = forward(4, 6, 3, 11, s_line, r_line, second(3))
    turn_keys = {r: [forward(2, 6, r, 8 + r, s_line, r_line, second(1))[0]] for r in (1, 2)}
    turn_values = {r: [forward(4, 6, r, 8 + r, s_line, r_line, second(3))[1]] for r in (1, 2)}
    q_copy = remote(qown, qraw, s_q, r_q, across)
    begin(ahead[1], ahead[3], right[0], left[0], ahead[2])
    pl.semaphore_wait(reach.at[0], 2)
    q_copy.start()
    qbuf[0] = arrange(qown[...])

    def scores(slot, chunk, part, queries):
        sbuf[part] = lax.dot_general(
            kbuf[slot, chunk], qbuf[queries], (((1,), (1,)), ((), ())),
            preferred_element_type=jnp.float32,
        )

    lead = lax.broadcasted_iota(jnp.int32, (SUF, COLS), 0)
    lane = lax.broadcasted_iota(jnp.int32, (SUF, COLS), 1)
    lead = lead - (lane // SUF * 8 + lane % 8)
    my_span = [span_ref[ctx], span_ref[place(1 - zh, u, w, c)]]

    def limit(slot, chunk, half, queries):
        return SUF * (my_span[queries] - span_ref[source_of(slot, chunk, half)])

    def absorb(slot, chunk, part, queries):
        pieces = []
        for half in range(2):
            base = half * KEYS
            pieces.append(sbuf[part, base : base + POOL])
            seen = lead <= limit(slot, chunk, half, queries)
            pieces.append(jnp.where(seen, sbuf[part, base + POOL : base + KEYS], NEG))
        peak = pieces[0].max(axis=0, keepdims=True)
        for piece in pieces[1:]:
            peak = jnp.maximum(peak, piece.max(axis=0, keepdims=True))
        old = top[queries, 0:1]
        new = jnp.maximum(old, peak * FACTOR)
        top[queries, 0:1] = new
        p = jnp.concatenate(
            [jnp.exp2(piece * FACTOR - new).astype(jnp.bfloat16) for piece in pieces], axis=0
        )
        acc[queries] = acc[queries] * jnp.exp2(old - new) + jnp.dot(
            vbuf[slot, chunk], p, preferred_element_type=jnp.float32
        )

    def sweep(count, pick, queries):
        scores(*pick(0, 0), 0, queries)
        if count == 1:
            scores(*pick(0, 1), 1, queries)
            absorb(*pick(0, 0), 0, queries)
            absorb(*pick(0, 1), 1, queries)
            return

        def pair(i, carry):
            later = jnp.minimum(i + 1, count - 1)
            scores(*pick(i, 1), 1, queries)
            absorb(*pick(i, 0), 0, queries)
            scores(*pick(later, 0), 0, queries)
            absorb(*pick(i, 1), 1, queries)
            return carry

        lax.fori_loop(0, count, pair, 0)

    def share(r, chunk):
        n = 2 * r + chunk
        rows = pl.ds(0, HEAD)
        return [
            remote(kbuf.at[2 * r, chunk], kbuf.at[2 * r + 1, chunk], s_core.at[n], r_core.at[n], partner),
            remote(vbuf.at[2 * r, chunk, rows], vbuf.at[2 * r + 1, chunk, rows], s_core.at[8 + n], r_core.at[8 + n], partner),
        ]

    core = [[share(r, chunk) for chunk in range(2)] for r in range(4)]
    def hop(source, *targets):
        for n in range(2):
            arrived(source[n : n + 1])
            begin(*[target[n : n + 1] for target in targets])

    hop(ahead[1], right[1], left[1])
    begin(core[0][0])
    hop(ahead[3], right[3], left[3])
    hop(ahead[2], right[2], left[2])
    begin(core[0][1])
    hop(right[0], turn_right)
    arrived(core[0][0])
    sweep(1, lambda i, j: (j, 0), 0)
    arrived(right[1][:1])
    begin(turn_keys[1])
    arrived(left[1][1:])
    begin(turn_values[1])
    hop(left[3], turn_left)
    arrived(right[1][1:])
    begin(core[1][0])
    arrived(left[0], left[1][:1])
    begin(core[2][0])
    arrived(core[0][1])
    sweep(1, lambda i, j: (j, 1), 0)
    sweep(1, lambda i, j: (2 + 2 * j, 0), 0)
    arrived(right[2][:1])
    begin(turn_keys[2])
    arrived(left[2][1:])
    begin(turn_values[2])
    arrived(left[2][:1])
    begin(core[2][1])
    arrived(right[2][1:], right[3])
    begin(core[1][1])
    arrived(core[1][0], core[2][0])
    sweep(1, lambda i, j: (3 + 2 * j, 0), 0)
    q_copy.wait_recv()
    qbuf[1] = arrange(qraw[...])
    sweep(2, lambda i, j: (i, j), 1)
    arrived(turn_right, turn_keys[1], turn_values[1])
    begin(core[3][0])
    arrived(core[1][1], core[2][1])
    sweep(2, lambda i, j: (2 + i, j), 1)
    arrived(turn_left, turn_keys[2], turn_values[2])
    begin(core[3][1])
    sweep(3, lambda i, j: (4 + i, j), 1)
    arrived(*core[3])
    sweep(1, lambda i, j: (7, j), 1)

    def finish(queries, order):
        total = acc[queries, HEAD : HEAD + 1]
        level = top[queries, 0:1] + jnp.log2(total)
        for z in range(HEADS):
            near = z // 2 * HEAD
            level_send[queries, z, 0:1] = level[:, near : near + HEAD]
        for step in order:
            begin(outs[queries, step][:1])
        flat[...] = (acc[queries, 0:HEAD] * (1.0 / total)).T
        for step in order:
            to = (zl + step) % HEADS
            send[queries, to] = flat[pl.ds(pl.multiple_of(to * SUF, SUF), SUF)].astype(jnp.bfloat16)
            begin(outs[queries, step][1:])

    outs = {}
    for n, (flip, step) in enumerate(far):
        who, to = column(flip, step), (zl + step) % HEADS
        row = pl.ds(0, 1)
        outs[flip, step] = [
            remote(level_send.at[flip, to, row], level_land.at[flip, zl, row], s_out.at[n], r_out.at[n], who),
            remote(send.at[flip, to], land.at[flip, zl], s_out.at[15 + n], r_out.at[15 + n], who),
        ]
    finish(1, (4, 3, 5, 2, 6, 1, 7, 0))
    sweep(2, lambda i, j: (2 + 2 * i + j, 1), 0)
    sweep(2, lambda i, j: (6 + i, j), 0)
    finish(0, (4, 3, 5, 2, 6, 1, 7))
    send[0, zl] = flat[pl.ds(pl.multiple_of(zl * SUF, SUF), SUF)].astype(jnp.bfloat16)
    land[0, zl] = send[0, zl]
    level_land[0, zl, 0:1] = level_send[0, zl, 0:1]
    arrived(*[copies[:1] for copies in outs.values()])

    def level_of(flip):
        return jnp.concatenate([level_land[flip, z, 0:1] for z in range(HEADS)], axis=0)

    near, other = level_of(0), level_of(1)
    peak = jnp.maximum(near, other)
    near, other = jnp.exp2(near - peak), jnp.exp2(other - peak)
    both = near + other
    weights[...] = jnp.concatenate([near / both, other / both], axis=0).T
    shares = weights[pl.ds(pl.multiple_of(zl % 2 * SUF, SUF), SUF)]
    for n in range(2 * HEADS):
        share_of[n] = jnp.broadcast_to(shares[:, n : n + 1], (SUF, HEAD))
    for step in (0, 4, 3, 5, 2, 6, 1, 7):
        z = (zl + HEADS - step) % HEADS
        arrived(outs[1, step][1:])
        if step:
            arrived(outs[0, step][1:])
        o = land[0, z].astype(jnp.float32) * share_of[z]
        o = o + land[1, z].astype(jnp.float32) * share_of[HEADS + z]
        row = jnp.concatenate([o[8 * g : 8 * g + 8] for g in range(GROUP)], axis=1)
        start = pl.multiple_of(z * GROUP * HEAD, GROUP * HEAD)
        out_ref[:, pl.ds(start, GROUP * HEAD)] = row.astype(jnp.bfloat16)

    q_copy.wait_send()
    for group in [*ahead.values(), *right, *left, turn_right, turn_left, *turn_keys.values(), *turn_values.values(), *core[0], *core[1], *core[2], *core[3], *outs.values()]:
        for copy in group:
            copy.wait_send()


def per_device(queries, suffix_keys, suffix_values, prefix_keys, prefix_values, counts, span_order):
    smem = pl.BlockSpec(memory_space=pltpu.SMEM)
    stays = pl.BlockSpec(memory_space=pltpu.HBM)
    vmem = pl.BlockSpec(memory_space=pltpu.VMEM)
    dma = pltpu.SemaphoreType.DMA
    bf16, f32 = jnp.bfloat16, jnp.float32
    return pl.pallas_call(
        kernel,
        out_shape=pltpu.VMEM((SUF // HEADS, HEADS * GROUP * HEAD), bf16),
        in_specs=[stays] * 5 + [smem] * 2,
        out_specs=vmem,
        scratch_shapes=[
            pltpu.VMEM((8, 2, WIDE, HEAD), bf16),
            pltpu.VMEM((8, 2, VROWS, WIDE), bf16),
            pltpu.VMEM((SUF, GROUP * HEAD), bf16),
            pltpu.VMEM((2, SUF, HEAD), bf16),
            pltpu.VMEM((2, POOL, HEAD), bf16),
            pltpu.VMEM((SUF, GROUP * HEAD), bf16),
            pltpu.VMEM((2, COLS, HEAD), bf16),
            pltpu.VMEM((2, WIDE, COLS), f32),
            pltpu.VMEM((2, VROWS, COLS), f32),
            pltpu.VMEM((2, 8, COLS), f32),
            pltpu.VMEM((2, HEADS, SUF, HEAD), bf16),
            pltpu.VMEM((2, HEADS, SUF, HEAD), bf16),
            pltpu.VMEM((2, HEADS, 8, HEAD), f32),
            pltpu.VMEM((2, HEADS, 8, HEAD), f32),
            pltpu.VMEM((COLS, HEAD), f32),
            pltpu.VMEM((2 * HEADS, SUF, HEAD), f32),
            pltpu.VMEM((HEAD, 2 * HEADS), f32),
            dma((6,)), dma((6,)), dma((24,)), dma((24,)), dma((16,)), dma((16,)),
            dma, dma, dma((30,)), dma((30,)), dma((5,)), pltpu.SemaphoreType.REGULAR((1,)),
        ],
        compiler_params=pltpu.CompilerParams(
            collective_id=0, has_side_effects=True, vmem_limit_bytes=LIMIT
        ),
    )(queries, suffix_keys, suffix_values, prefix_keys, prefix_values, counts, span_order)


def solution(mesh):
    two = P("ctx", "head")
    return jax.shard_map(
        per_device,
        mesh=mesh,
        in_specs=(two, two, two, two, two, P(), P()),
        out_specs=P(("ctx", "head"), None),
        check_vma=False,
    )
```

```python
import math

import jax
import jax.numpy as jnp
from jax import lax
from jax.experimental import pallas as pl
from jax.experimental.pallas import tpu as pltpu
from jax.sharding import PartitionSpec as P

HEAD = 128
GROUP = 8
SUF = 64
POOL = 320
KEYS = POOL + SUF
WIDE = 2 * KEYS
VROWS = 144
COLS = SUF * GROUP
LIMIT = 63 << 20
SIDE = 4
HEADS = 8
NEG = -1e30
FACTOR = math.log2(math.e) / math.sqrt(HEAD)
MESH = pl.DeviceIdType.MESH


def kernel(
    q_ref, sk_ref, sv_ref, pk_ref, pv_ref, count_ref, span_ref, out_ref,
    kbuf, vbuf, qown, skv, pkv, qraw, qbuf, sbuf, acc, top, send, land, level_send, level_land, flat, share_of, weights,
    s_first, r_first, s_line, r_line, s_core, r_core, s_q, r_q, s_out, r_out, s_own, reach,
):
    ctx, zl = lax.axis_index("ctx"), lax.axis_index("head")
    c = ctx % 2
    x = ctx // 2 % SIDE
    y = ctx // (2 * SIDE) % SIDE
    zh = ctx // (2 * SIDE * SIDE)
    u = y * (1 - c) + x * c
    w = x * (1 - c) + y * c

    def place(plane, first, second, core):
        row = first * (1 - core) + second * core
        col = second * (1 - core) + first * core
        return ((plane * SIDE + row) * SIDE + col) * 2 + core

    def first(step):
        return (place(zh, (u + step) % SIDE, w, c), zl)

    def second(step):
        return (place(zh, u, (w + step) % SIDE, c), zl)

    partner = (ctx + 1 - 2 * c, zl)
    across = (place(1 - zh, u, w, c), zl)

    def column(flip, step):
        plane = (zh + flip) % 2
        return (place(plane, u, w, c), (zl + step) % HEADS)

    far = [(flip, step) for flip in (1, 0) for step in (4, 3, 5, 2, 6, 1, 7, 0) if flip or step]

    barrier = pltpu.get_barrier_semaphore()

    def along(step):
        z = (zh * HEADS + zl + step) % (2 * HEADS)
        return (place(z // HEADS, u, w, c), z % HEADS)

    greeted = [first(1), first(2), first(3), second(1), second(3), partner]
    greeted += [along(step) for k in (1, 2, 3, 4) for step in (k, 16 - k)]
    for who in greeted:
        pl.semaphore_signal(barrier, inc=1, device_id=who, device_id_type=MESH)

    def remote(src, dst, s_sem, r_sem, who):
        return pltpu.make_async_remote_copy(
            src_ref=src, dst_ref=dst, send_sem=s_sem, recv_sem=r_sem,
            device_id=who, device_id_type=MESH,
        )

    loads = [
        pltpu.make_async_copy(source, target, s_own.at[n])
        for n, (source, target) in enumerate(
            [(pk_ref, pkv.at[0]), (sk_ref, skv.at[0]), (pv_ref, pkv.at[1]), (sv_ref, skv.at[1]), (q_ref, qown)]
        )
    ]
    for load in loads:
        load.start()

    def arrange(block):
        block = block.astype(jnp.float32)
        rows = [
            block[8 * z : 8 * z + 8, HEAD * g : HEAD * (g + 1)]
            for z in range(HEADS)
            for g in range(GROUP)
        ]
        return jnp.concatenate(rows, axis=0).astype(jnp.bfloat16)

    acc[...] = jnp.zeros_like(acc)
    top[...] = jnp.full(top.shape, NEG, jnp.float32)

    def batch_of(slot):
        rank = slot // 2
        return rank + rank // 2 - rank // 3 * 2

    def source_of(slot, chunk, half):
        whose = slot % 2
        core = c + whose - 2 * c * whose
        uu = u * (1 - whose) + w * whose
        ww = w * (1 - whose) + u * whose
        relative = chunk * 2 + half
        return place(zh, (uu - relative + SIDE) % SIDE, (ww - batch_of(slot) + SIDE) % SIDE, core)

    one_row = lax.broadcasted_iota(jnp.int32, (VROWS - HEAD, KEYS), 0)
    one_col = lax.broadcasted_iota(jnp.int32, (VROWS - HEAD, KEYS), 1)

    def ones_of(slot, carry):
        for chunk in range(2):
            for half in range(2):
                count = count_ref[source_of(slot, chunk, half)]
                row = jnp.where((one_row == 0) & ((one_col < count) | (one_col >= POOL)), 1.0, 0.0)
                vbuf[slot, chunk, HEAD:VROWS, half * KEYS : (half + 1) * KEYS] = row.astype(jnp.bfloat16)
        return carry

    lax.fori_loop(0, 8, ones_of, 0)

    for load in loads:
        load.wait()
    live = lax.broadcasted_iota(jnp.int32, (POOL, HEAD), 0) < count_ref[ctx]
    rows = pkv[0].astype(jnp.float32)
    kbuf[0, 0, 0:POOL] = jnp.where(live, rows, rows[0:1]).astype(jnp.bfloat16)
    kbuf[0, 0, POOL:KEYS] = skv[0]
    rows = jnp.where(live, pkv[1].astype(jnp.float32), 0.0)
    rows = jnp.concatenate([rows, skv[1].astype(jnp.float32)], axis=0)
    vbuf[0, 0, 0:HEAD, 0:KEYS] = rows.T.astype(jnp.bfloat16)

    pl.semaphore_wait(barrier, len(greeted))
    for step in (4, 12):
        pl.semaphore_signal(reach.at[0], inc=1, device_id=along(step), device_id_type=MESH)

    def keys_at(slot, piece):
        return kbuf.at[slot, piece // 2, pl.ds(piece % 2 * KEYS, KEYS)]

    def values_at(slot, piece):
        return vbuf.at[slot, piece // 2, pl.ds(0, HEAD), pl.ds(piece % 2 * KEYS, KEYS)]

    def forward(source, target, piece, n, s_sem, r_sem, who):
        begins = 0 if s_sem is s_first else piece
        return [
            remote(keys_at(source, begins), keys_at(target, piece), s_sem.at[2 * n], r_sem.at[2 * n], who),
            remote(values_at(source, begins), values_at(target, piece), s_sem.at[2 * n + 1], r_sem.at[2 * n + 1], who),
        ]

    def begin(*groups):
        for group in groups:
            for copy in group:
                copy.start()

    def arrived(*groups):
        for group in groups:
            for copy in group:
                copy.wait_recv()

    ahead = {r: forward(0, 0, r, r - 1, s_first, r_first, first(r)) for r in (1, 3, 2)}
    right = [forward(0, 2, r, r, s_line, r_line, second(1)) for r in range(4)]
    left = [forward(0, 4, r, 4 + r, s_line, r_line, second(3)) for r in range(4)]
    turn_right = forward(2, 6, 0, 8, s_line, r_line, second(1))
    turn_left = forward(4, 6, 3, 11, s_line, r_line, second(3))
    turn_keys = {r: [forward(2, 6, r, 8 + r, s_line, r_line, second(1))[0]] for r in (1, 2)}
    turn_values = {r: [forward(4, 6, r, 8 + r, s_line, r_line, second(3))[1]] for r in (1, 2)}
    q_copy = remote(qown, qraw, s_q, r_q, across)
    begin(ahead[1], ahead[3], right[0], left[0], ahead[2])
    pl.semaphore_wait(reach.at[0], 2)
    q_copy.start()
    qbuf[0] = arrange(qown[...])

    def scores(slot, chunk, part, queries):
        sbuf[part] = lax.dot_general(
            kbuf[slot, chunk], qbuf[queries], (((1,), (1,)), ((), ())),
            preferred_element_type=jnp.float32,
        )

    lead = lax.broadcasted_iota(jnp.int32, (SUF, COLS), 0)
    lane = lax.broadcasted_iota(jnp.int32, (SUF, COLS), 1)
    lead = lead - (lane // SUF * 8 + lane % 8)
    my_span = [span_ref[ctx], span_ref[place(1 - zh, u, w, c)]]

    def limit(slot, chunk, half, queries):
        return SUF * (my_span[queries] - span_ref[source_of(slot, chunk, half)])

    def absorb(slot, chunk, part, queries):
        pieces = []
        for half in range(2):
            base = half * KEYS
            pieces.append(sbuf[part, base : base + POOL])
            seen = lead <= limit(slot, chunk, half, queries)
            pieces.append(jnp.where(seen, sbuf[part, base + POOL : base + KEYS], NEG))
        peak = pieces[0].max(axis=0, keepdims=True)
        for piece in pieces[1:]:
            peak = jnp.maximum(peak, piece.max(axis=0, keepdims=True))
        old = top[queries, 0:1]
        new = jnp.maximum(old, peak * FACTOR)
        top[queries, 0:1] = new
        p = jnp.concatenate(
            [jnp.exp2(piece * FACTOR - new).astype(jnp.bfloat16) for piece in pieces], axis=0
        )
        acc[queries] = acc[queries] * jnp.exp2(old - new) + jnp.dot(
            vbuf[slot, chunk], p, preferred_element_type=jnp.float32
        )

    def sweep(count, pick, queries):
        scores(*pick(0, 0), 0, queries)
        if count == 1:
            scores(*pick(0, 1), 1, queries)
            absorb(*pick(0, 0), 0, queries)
            absorb(*pick(0, 1), 1, queries)
            return

        def pair(i, carry):
            later = jnp.minimum(i + 1, count - 1)
            scores(*pick(i, 1), 1, queries)
            absorb(*pick(i, 0), 0, queries)
            scores(*pick(later, 0), 0, queries)
            absorb(*pick(i, 1), 1, queries)
            return carry

        lax.fori_loop(0, count, pair, 0)

    def share(r, chunk):
        n = 2 * r + chunk
        rows = pl.ds(0, HEAD)
        return [
            remote(kbuf.at[2 * r, chunk], kbuf.at[2 * r + 1, chunk], s_core.at[n], r_core.at[n], partner),
            remote(vbuf.at[2 * r, chunk, rows], vbuf.at[2 * r + 1, chunk, rows], s_core.at[8 + n], r_core.at[8 + n], partner),
        ]

    core = [[share(r, chunk) for chunk in range(2)] for r in range(4)]
    def hop(source, *targets):
        for n in range(2):
            arrived(source[n : n + 1])
            begin(*[target[n : n + 1] for target in targets])

    hop(ahead[1], right[1], left[1])
    begin(core[0][0])
    hop(ahead[3], right[3], left[3])
    hop(ahead[2], right[2], left[2])
    begin(core[0][1])
    hop(right[0], turn_right)
    arrived(core[0][0])
    sweep(1, lambda i, j: (j, 0), 0)
    arrived(right[1][:1])
    begin(turn_keys[1])
    arrived(left[1][1:])
    begin(turn_values[1])
    hop(left[3], turn_left)
    arrived(right[1][1:])
    begin(core[1][0])
    arrived(left[0], left[1][:1])
    begin(core[2][0])
    arrived(core[0][1])
    sweep(1, lambda i, j: (j, 1), 0)
    sweep(1, lambda i, j: (2 + 2 * j, 0), 0)
    arrived(right[2][:1])
    begin(turn_keys[2])
    arrived(left[2][1:])
    begin(turn_values[2])
    arrived(left[2][:1])
    begin(core[2][1])
    arrived(right[2][1:], right[3])
    begin(core[1][1])
    arrived(core[1][0], core[2][0])
    q_copy.wait_recv()
    qbuf[1] = arrange(qraw[...])
    sweep(2, lambda i, j: (i, j), 1)
    arrived(turn_right, turn_keys[1], turn_values[1])
    begin(core[3][0])
    arrived(core[1][1], core[2][1])
    sweep(2, lambda i, j: (2 + i, j), 1)
    arrived(turn_left, turn_keys[2], turn_values[2])
    begin(core[3][1])
    sweep(3, lambda i, j: (4 + i, j), 1)
    arrived(*core[3])
    sweep(1, lambda i, j: (7, j), 1)

    def finish(queries, order):
        total = acc[queries, HEAD : HEAD + 1]
        level = top[queries, 0:1] + jnp.log2(total)
        for z in range(HEADS):
            near = z // 2 * HEAD
            level_send[queries, z, 0:1] = level[:, near : near + HEAD]
        for step in order:
            begin(outs[queries, step][:1])
        flat[...] = (acc[queries, 0:HEAD] * (1.0 / total)).T
        for step in order:
            to = (zl + step) % HEADS
            send[queries, to] = flat[pl.ds(pl.multiple_of(to * SUF, SUF), SUF)].astype(jnp.bfloat16)
            begin(outs[queries, step][1:])

    outs = {}
    for n, (flip, step) in enumerate(far):
        who, to = column(flip, step), (zl + step) % HEADS
        row = pl.ds(0, 1)
        outs[flip, step] = [
            remote(level_send.at[flip, to, row], level_land.at[flip, zl, row], s_out.at[n], r_out.at[n], who),
            remote(send.at[flip, to], land.at[flip, zl], s_out.at[15 + n], r_out.at[15 + n], who),
        ]
    finish(1, (4, 3, 5, 2, 6, 1, 7, 0))
    sweep(1, lambda i, j: (3 + 2 * j, 0), 0)
    sweep(2, lambda i, j: (2 + 2 * i + j, 1), 0)
    sweep(2, lambda i, j: (6 + i, j), 0)
    finish(0, (4, 3, 5, 2, 6, 1, 7))
    send[0, zl] = flat[pl.ds(pl.multiple_of(zl * SUF, SUF), SUF)].astype(jnp.bfloat16)
    land[0, zl] = send[0, zl]
    level_land[0, zl, 0:1] = level_send[0, zl, 0:1]
    arrived(*[copies[:1] for copies in outs.values()])

    def level_of(flip):
        return jnp.concatenate([level_land[flip, z, 0:1] for z in range(HEADS)], axis=0)

    near, other = level_of(0), level_of(1)
    peak = jnp.maximum(near, other)
    near, other = jnp.exp2(near - peak), jnp.exp2(other - peak)
    both = near + other
    weights[...] = jnp.concatenate([near / both, other / both], axis=0).T
    shares = weights[pl.ds(pl.multiple_of(zl % 2 * SUF, SUF), SUF)]
    for n in range(2 * HEADS):
        share_of[n] = jnp.broadcast_to(shares[:, n : n + 1], (SUF, HEAD))
    for step in (0, 4, 3, 5, 2, 6, 1, 7):
        z = (zl + HEADS - step) % HEADS
        arrived(outs[1, step][1:])
        if step:
            arrived(outs[0, step][1:])
        o = land[0, z].astype(jnp.float32) * share_of[z]
        o = o + land[1, z].astype(jnp.float32) * share_of[HEADS + z]
        row = jnp.concatenate([o[8 * g : 8 * g + 8] for g in range(GROUP)], axis=1)
        start = pl.multiple_of(z * GROUP * HEAD, GROUP * HEAD)
        out_ref[:, pl.ds(start, GROUP * HEAD)] = row.astype(jnp.bfloat16)

    q_copy.wait_send()
    for group in [*ahead.values(), *right, *left, turn_right, turn_left, *turn_keys.values(), *turn_values.values(), *core[0], *core[1], *core[2], *core[3], *outs.values()]:
        for copy in group:
            copy.wait_send()


def per_device(queries, suffix_keys, suffix_values, prefix_keys, prefix_values, counts, span_order):
    smem = pl.BlockSpec(memory_space=pltpu.SMEM)
    stays = pl.BlockSpec(memory_space=pltpu.HBM)
    vmem = pl.BlockSpec(memory_space=pltpu.VMEM)
    dma = pltpu.SemaphoreType.DMA
    bf16, f32 = jnp.bfloat16, jnp.float32
    return pl.pallas_call(
        kernel,
        out_shape=pltpu.VMEM((SUF // HEADS, HEADS * GROUP * HEAD), bf16),
        in_specs=[stays] * 5 + [smem] * 2,
        out_specs=vmem,
        scratch_shapes=[
            pltpu.VMEM((8, 2, WIDE, HEAD), bf16),
            pltpu.VMEM((8, 2, VROWS, WIDE), bf16),
            pltpu.VMEM((SUF, GROUP * HEAD), bf16),
            pltpu.VMEM((2, SUF, HEAD), bf16),
            pltpu.VMEM((2, POOL, HEAD), bf16),
            pltpu.VMEM((SUF, GROUP * HEAD), bf16),
            pltpu.VMEM((2, COLS, HEAD), bf16),
            pltpu.VMEM((2, WIDE, COLS), f32),
            pltpu.VMEM((2, VROWS, COLS), f32),
            pltpu.VMEM((2, 8, COLS), f32),
            pltpu.VMEM((2, HEADS, SUF, HEAD), bf16),
            pltpu.VMEM((2, HEADS, SUF, HEAD), bf16),
            pltpu.VMEM((2, HEADS, 8, HEAD), f32),
            pltpu.VMEM((2, HEADS, 8, HEAD), f32),
            pltpu.VMEM((COLS, HEAD), f32),
            pltpu.VMEM((2 * HEADS, SUF, HEAD), f32),
            pltpu.VMEM((HEAD, 2 * HEADS), f32),
            dma((6,)), dma((6,)), dma((24,)), dma((24,)), dma((16,)), dma((16,)),
            dma, dma, dma((30,)), dma((30,)), dma((5,)), pltpu.SemaphoreType.REGULAR((1,)),
        ],
        compiler_params=pltpu.CompilerParams(
            collective_id=0, has_side_effects=True, vmem_limit_bytes=LIMIT
        ),
    )(queries, suffix_keys, suffix_values, prefix_keys, prefix_values, counts, span_order)


def solution(mesh):
    two = P("ctx", "head")
    return jax.shard_map(
        per_device,
        mesh=mesh,
        in_specs=(two, two, two, two, two, P(), P()),
        out_specs=P(("ctx", "head"), None),
        check_vma=False,
    )
```
